32 devices in a mesh: walk: 4 (over y, core), stretch: 8 (over z, x).
Axes of the slice: x: 2, y: 2, z: 4, core: 2. Of those that a mesh axis runs over, the one named last changes fastest.
Arguments:
- walkers: float32 [64, 48, 512], P(('walk', 'stretch')), may hold values from -6 to 6
- inverse_intersection: float32 [64, 48, 48], P(('walk', 'stretch')), may hold values from -0.875 to 0.875
- half_rotated: bfloat16 [1024, 48, 512], P('stretch'), may hold values from -0.076546554 to 0.076546554
- cholesky: bfloat16 [1024, 512, 512], P('stretch'), may hold values from -0.015625 to 0.015625
- field_noise: float32 [64, 1024], P('walk', 'stretch'), may hold values from -6 to 6
- branch_sources: int32 [64], P(('walk', 'stretch')), may hold values from 0 to 63, as said below
Outputs:
- force_bias: float32 [64, 1024], P('walk', 'stretch')
- exchange_energy: float32 [64], P(('walk', 'stretch'))
- new_walkers: float32 [64, 48, 512], P(('walk', 'stretch'))
The draws below stay inside these ranges and needn't reach their ends.
Inputs may be any that keep to these rules, and one draw needn't show every extreme that they name: `branch_sources`: walker d lies in column (d // 2) % 8; every entry names a walker of the same column as its destination slot. A walker may be named by several slots or by none.
All inputs are finite; a program needn't handle non-finite values.
Results may differ from the reference program's by a relative error of at most 0.0029.
Values may be sent and summed in bfloat16 or wider, within the bound.
A program may use at most 320 MiB of HBM per device.

```python
import math
import jax
import jax.numpy as jnp
from jax import lax

M = 512
NOCC = 48
NCHOL = 1024
WD = 2
ORDERS = 2
GROUP_WALKERS = 16
WALKERS = 64


def draw_half_rotated(key, part):
    ramp = 1.0 + 2.0 * jnp.arange(NCHOL, dtype=jnp.float32) / NCHOL
    base = jax.random.truncated_normal(key, -4.0, 4.0, (NCHOL, NOCC, M), jnp.float32)
    values = base * ramp[:, None, None] / math.sqrt(NOCC * M)
    return values.astype(jnp.bfloat16)


def draw_branch_sources(key, part):
    first, second, third = jax.random.split(jax.random.fold_in(key, 7), 3)
    walk_count = WALKERS // GROUP_WALKERS
    destination = jnp.arange(WALKERS, dtype=jnp.int32)
    column = destination // WD % (GROUP_WALKERS // WD)
    walk_one = jax.random.randint(first, (WALKERS,), 0, walk_count, dtype=jnp.int32)
    walk_two = jax.random.randint(second, (WALKERS,), 0, walk_count, dtype=jnp.int32)
    local_row = jax.random.randint(third, (WALKERS,), 0, WD, dtype=jnp.int32)
    source = jnp.minimum(walk_one, walk_two) * GROUP_WALKERS + column * WD + local_row
    source = source.at[0].set(0).at[WALKERS - 1].set(WALKERS - 1)
    return source.astype(jnp.int32)


def levels(stream_key, dims, cuts, smallest, top_value):
    level, own = 1.0, jax.random.fold_in(stream_key, 6)
    for dim, parts in cuts:
        heights = jnp.exp(jax.random.uniform(jax.random.fold_in(own, dim), (parts,), jnp.float32, smallest / len(cuts), top_value / len(cuts)))
        level = level * jnp.repeat(heights, dims[dim] // parts).reshape([-1 if axis == dim else 1 for axis in range(len(dims))])
    return level


def scatter_about(key, shape, scale, limit, shards=(), held_as=jnp.bfloat16):
    level = levels(key, shape, shards, -0.22, 0.18) if shards else 1.0
    entries = jax.random.normal(key, shape, jnp.float32) * scale * level
    return jnp.minimum(jnp.maximum(entries, -limit), limit).astype(held_as)


def setup_inputs(seed: int = 0) -> dict:
    key_of = jax.random.split(jax.random.key(seed), 7)
    walkers = scatter_about(key_of[0], (WALKERS, NOCC, M), 1.0, 6.0, ((0, 32),), jnp.float32)
    inverse_intersection = scatter_about(key_of[1], (WALKERS, NOCC, NOCC), NOCC ** -0.5, 0.875, ((0, 32),), jnp.float32)
    half_rotated = draw_half_rotated(jax.random.fold_in(key_of[6], 71), 0)
    cholesky = scatter_about(key_of[3], (NCHOL, M, M), (2.0 / (M * NCHOL) ** 0.5), 0.015625, ((0, 8),))
    field_noise = scatter_about(key_of[4], (WALKERS, NCHOL), 1.0, 6.0, ((0, 4), (1, 8)), jnp.float32)
    branch_sources = draw_branch_sources(jax.random.fold_in(key_of[6], 71), 0)
    return dict(walkers=walkers, inverse_intersection=inverse_intersection, half_rotated=half_rotated, cholesky=cholesky, field_noise=field_noise, branch_sources=branch_sources)


def reference(walkers, inverse_intersection, half_rotated, cholesky, field_noise, branch_sources):
    green = jnp.einsum("wij,wjp->wip", inverse_intersection, walkers, precision=lax.Precision.HIGHEST).astype(jnp.bfloat16)
    hr_flat = half_rotated.reshape(NCHOL * NOCC, M)
    step_rows = math.gcd(WALKERS, 4)

    def contract(green_block):
        intersections = lax.dot_general(hr_flat, green_block.reshape(step_rows * NOCC, M), (((1,), (1,)), ((), ())), preferred_element_type=jnp.float32)
        intersections = intersections.reshape(NCHOL, NOCC, step_rows, NOCC)
        bias_block = 2.0 * jnp.trace(intersections, axis1=1, axis2=3).T
        energy_block = -0.5 * jnp.sum(intersections * jnp.transpose(intersections, (0, 3, 2, 1)), axis=(0, 1, 3))
        return bias_block, energy_block

    bias_blocks, energy_blocks = lax.map(contract, green.reshape(WALKERS // step_rows, step_rows, NOCC, M))
    force_bias = bias_blocks.reshape(WALKERS, NCHOL)
    exchange_energy = energy_blocks.reshape(WALKERS)
    fields = (0.05 * (field_noise - force_bias)).astype(jnp.bfloat16)
    chol_flat = cholesky.reshape(NCHOL, M * M)
    block_size = math.gcd(WALKERS, 16)

    def one_block(operands):
        psi_block, field_block = operands
        matrix = jnp.dot(field_block, chol_flat, preferred_element_type=jnp.float32).reshape(block_size, M, M)
        return jnp.einsum("bip,bpq->biq", psi_block.astype(jnp.float32), matrix, precision=lax.Precision.HIGHEST)

    term = walkers
    propagated = walkers
    for degree in range(1, ORDERS + 1):
        rows_now = term.astype(jnp.bfloat16)
        summed = lax.map(one_block, (rows_now.reshape(WALKERS // block_size, block_size, NOCC, M), fields.reshape(WALKERS // block_size, block_size, NCHOL)))
        term = summed.reshape(WALKERS, NOCC, M) / degree
        propagated = propagated + term
    new_walkers = jnp.take(propagated, branch_sources, axis=0)
    return force_bias, exchange_energy, new_walkers
```

```python
import functools
import math

import jax
import jax.numpy as jnp
from jax import lax
from jax.experimental import pallas as pl
from jax.experimental.pallas import tpu as pltpu
from jax.sharding import PartitionSpec as P

ORDERS = 2
ROWS = 16
MESH = pl.DeviceIdType.MESH
VMEM = pltpu.VMEM
LIMIT = 60 * 2**20


def around(axis, n, me, d):
    return {axis: lax.rem(me + d, n)}


def send(src, dst, sems, stage, d, device):
    return pltpu.make_async_remote_copy(
        src_ref=src,
        dst_ref=dst,
        send_sem=sems[0].at[stage, d - 1],
        recv_sem=sems[1].at[stage, d - 1],
        device_id=device,
        device_id_type=MESH,
    )


def greet(axes):
    barrier = pltpu.get_barrier_semaphore()
    total = 0
    for axis, n, me in axes:
        for d in range(1, n):
            pl.semaphore_signal(barrier, inc=1, device_id=around(axis, n, me, d), device_id_type=MESH)
        total += n - 1
    pl.semaphore_wait(barrier, total)


def green_kernel(n, inverse_ref, walkers_ref, out_ref, mine, landed, send_sem, recv_sem):
    me = lax.axis_index("stretch")
    sems = (send_sem, recv_sem)
    for k in range(walkers_ref.shape[0]):
        mine[k] = jnp.dot(
            inverse_ref[k],
            walkers_ref[k],
            precision=lax.Precision.HIGHEST,
            preferred_element_type=jnp.float32,
        ).astype(jnp.bfloat16)
    greet([("stretch", n, me)])
    copies = []
    for d in range(1, n):
        copy = send(mine, landed.at[me], sems, 0, d, around("stretch", n, me, d))
        copy.start()
        copies.append(copy)
    out_ref[me] = mine[...]
    for d in range(1, n):
        copies[d - 1].wait()
        source = lax.rem(me - d + n, n)
        out_ref[source] = landed[source]


def gather_green(inverse, walkers, n):
    shape = walkers.shape
    return pl.pallas_call(
        functools.partial(green_kernel, n),
        out_shape=jax.ShapeDtypeStruct((n, *shape), jnp.bfloat16),
        in_specs=[pl.BlockSpec(memory_space=VMEM)] * 2,
        out_specs=pl.BlockSpec(memory_space=VMEM),
        scratch_shapes=[
            VMEM(shape, jnp.bfloat16),
            VMEM((n, *shape), jnp.bfloat16),
            pltpu.SemaphoreType.DMA((1, n - 1)),
            pltpu.SemaphoreType.DMA((1, n - 1)),
        ],
        compiler_params=pltpu.CompilerParams(
            collective_id=0, has_side_effects=True, vmem_limit_bytes=LIMIT
        ),
    )(inverse, walkers)


def bias_kernel(green_ref, rotated_ref, noise_ref, bias_ref, fields_ref, energy_ref, inter):
    step = pl.program_id(1)
    occupied, block, orbitals = green_ref.shape
    span, vectors, _ = rotated_ref.shape
    green = green_ref[...].reshape(occupied * block, orbitals)
    for i in range(0, span, 2):
        part = lax.dot_general(
            green,
            rotated_ref[i : i + 2].reshape(2 * vectors, orbitals),
            (((1,), (1,)), ((), ())),
            preferred_element_type=jnp.float32,
        )
        for k in range(2):
            inter[step * span + i + k] = part[:, k * vectors : (k + 1) * vectors].reshape(
                occupied, block, vectors
            )

    @pl.when(step == pl.num_programs(1) - 1)
    def _():
        def one(i, carry):
            energy, trace = carry
            energy = energy + jnp.sum(inter[i] * inter[:, i], axis=0)
            return energy, trace + inter[i, i]

        zero = jnp.zeros((block, vectors), jnp.float32)
        energy, trace = lax.fori_loop(0, occupied, one, (zero, zero))
        bias = 2.0 * trace
        bias_ref[...] = bias
        fields_ref[...] = (0.05 * (noise_ref[...] - bias)).astype(jnp.bfloat16).astype(jnp.float32)
        share = -0.5 * jnp.sum(energy, axis=1, keepdims=True)
        energy_ref[...] = jnp.broadcast_to(share[:, :, None], energy_ref.shape)


def bias_and_energy(green, rotated, noise):
    occupied, group, orbitals = green.shape
    vectors = rotated.shape[1]
    block = math.gcd(group, 16)
    span = 8
    grid = (group // block, occupied // span)
    return pl.pallas_call(
        bias_kernel,
        grid=grid,
        out_shape=(
            jax.ShapeDtypeStruct((group, vectors), jnp.float32),
            jax.ShapeDtypeStruct((group, vectors), jnp.float32),
            jax.ShapeDtypeStruct((group, 8, 128), jnp.float32),
        ),
        in_specs=[
            pl.BlockSpec((occupied, block, orbitals), lambda w, i: (0, w, 0)),
            pl.BlockSpec((span, vectors, orbitals), lambda w, i: (i, 0, 0)),
            pl.BlockSpec((block, vectors), lambda w, i: (w, 0)),
        ],
        out_specs=(
            pl.BlockSpec((block, vectors), lambda w, i: (w, 0)),
            pl.BlockSpec((block, vectors), lambda w, i: (w, 0)),
            pl.BlockSpec((block, 8, 128), lambda w, i: (w, 0, 0)),
        ),
        scratch_shapes=[VMEM((occupied, occupied, block, vectors), jnp.float32)],
        compiler_params=pltpu.CompilerParams(vmem_limit_bytes=LIMIT),
    )(green, rotated, noise)


def propagate_kernel(
    n,
    columns,
    fields_ref,
    energy_in,
    rows_ref,
    walkers_ref,
    chol_ref,
    out_ref,
    energy_ref,
    spread,
    matrix,
    rows_all,
    rows_next,
    outgoing,
    landed_one,
    landed_two,
    energy_landed,
    column_walkers,
    column_terms,
    terms,
    total,
    send_sem,
    recv_sem,
    column_send,
    column_recv,
):
    me = lax.axis_index("stretch")
    seat = lax.axis_index("walk")
    step = pl.program_id(0)
    last = pl.num_programs(0) - 1
    vectors, span, orbitals = chol_ref.shape
    group = fields_ref.shape[0]
    count = rows_ref.shape[0]
    sems = (send_sem, recv_sem)
    column_sems = (column_send, column_recv)

    def first_sends():
        copies = []
        for d in range(1, n):
            to = around("stretch", n, me, d)
            there = lax.rem(me + d, n)
            copies.append(send(rows_ref, rows_all.at[me], sems, 0, d, to))
            copies.append(send(energy_in.at[there], energy_landed.at[me], sems, 1, d, to))
        for d in range(1, columns):
            to = around("walk", columns, seat, d)
            copies.append(send(walkers_ref, column_walkers.at[seat], column_sems, 0, d, to))
        return copies

    @pl.when(step == 0)
    def _():
        greet([("stretch", n, me), ("walk", columns, seat)])
        for copy in first_sends():
            copy.start()
        wide = vectors * ROWS
        column = lax.broadcasted_iota(jnp.int32, (vectors, wide), 1)
        row = lax.broadcasted_iota(jnp.int32, (vectors, wide), 0)
        repeat = jnp.where(column // ROWS == row, 1.0, 0.0).astype(jnp.bfloat16)
        repeated = jnp.dot(
            fields_ref[...].astype(jnp.bfloat16), repeat, preferred_element_type=jnp.float32
        )
        place = lax.broadcasted_iota(jnp.int32, (ROWS, wide), 0)
        where = lax.broadcasted_iota(jnp.int32, (ROWS, wide), 1) % ROWS
        for w in range(group):
            line = jnp.broadcast_to(repeated[w : w + 1], (ROWS, wide))
            spread[w * ROWS : (w + 1) * ROWS] = jnp.where(place == where, line, 0.0).astype(
                jnp.bfloat16
            )

    for c in range(span // ROWS):
        product = jnp.dot(
            spread[...],
            chol_ref[:, c * ROWS : (c + 1) * ROWS, :].reshape(vectors * ROWS, orbitals),
            preferred_element_type=jnp.float32,
        )
        start = pl.multiple_of(step * span + c * ROWS, ROWS)
        matrix[:, pl.ds(start, ROWS), :] = product.astype(jnp.bfloat16).reshape(
            group, ROWS, orbitals
        )

    @pl.when(step == last)
    def _():
        def apply(rows, owner, k):
            return jnp.dot(
                rows[owner, k], matrix[owner * count + k], preferred_element_type=jnp.float32
            )

        for copy in first_sends():
            copy.wait()
        rows_all[me] = rows_ref[...]
        column_walkers[seat] = walkers_ref[...]
        energy = energy_in[me]
        for d in range(1, n):
            energy = energy + energy_landed[lax.rem(me - d + n, n)]
        energy_ref[...] = energy

        copies = []
        for d in range(1, n):
            owner = lax.rem(me + d, n)
            for k in range(count):
                outgoing[owner, k] = apply(rows_all, owner, k).astype(jnp.bfloat16)
            copy = send(
                outgoing.at[owner], landed_one.at[me], sems, 2, d, around("stretch", n, me, d)
            )
            copy.start()
            copies.append(copy)
        for k in range(count):
            total[k] = apply(rows_all, me, k)
        for d in range(1, n):
            copies[d - 1].wait()
            total[...] += landed_one[lax.rem(me - d + n, n)].astype(jnp.float32)
        rows_next[me] = total[...].astype(jnp.bfloat16)
        copies = []
        for d in range(1, n):
            copy = send(
                rows_next.at[me], rows_next.at[me], sems, 3, d, around("stretch", n, me, d)
            )
            copy.start()
            copies.append(copy)
        second = [0.5 * apply(rows_next, me, k) for k in range(count)]
        for k in range(count):
            total[k] += second[k]
        backs = []
        for d in range(1, n):
            copies[d - 1].wait()
            owner = lax.rem(me - d + n, n)
            for k in range(count):
                outgoing[owner, k] = (0.5 * apply(rows_next, owner, k)).astype(jnp.bfloat16)
            copy = send(
                outgoing.at[owner], landed_two.at[me], sems, 4, d, around("stretch", n, me, n - d)
            )
            copy.start()
            backs.append(copy)
        for d in range(1, n):
            backs[d - 1].wait()
            total[...] += landed_two[lax.rem(me + d, n)].astype(jnp.float32)
        terms[...] = total[...].astype(jnp.bfloat16)
        copies = []
        for d in range(1, columns):
            copy = send(
                terms,
                column_terms.at[seat],
                column_sems,
                1,
                d,
                around("walk", columns, seat, d),
            )
            copy.start()
            copies.append(copy)
        out_ref[seat] = walkers_ref[...] + total[...]
        for d in range(1, columns):
            copies[d - 1].wait()
            source = lax.rem(seat - d + columns, columns)
            out_ref[source] = column_walkers[source] + column_terms[source].astype(jnp.float32)


def propagate(fields, energy, walkers, cholesky, n, columns):
    count, occupied, orbitals = walkers.shape
    group, vectors = fields.shape
    span = 2 * ROWS
    shape = (count, occupied, orbitals)
    whole = pl.BlockSpec(memory_space=VMEM)
    half = jnp.bfloat16
    return pl.pallas_call(
        functools.partial(propagate_kernel, n, columns),
        grid=(orbitals // span,),
        out_shape=(
            jax.ShapeDtypeStruct((columns, *shape), jnp.float32),
            jax.ShapeDtypeStruct((count, 8, 128), jnp.float32),
        ),
        in_specs=[
            whole,
            whole,
            whole,
            whole,
            pl.BlockSpec((vectors, span, orbitals), lambda p: (0, p, 0)),
        ],
        out_specs=(whole, whole),
        scratch_shapes=[
            VMEM((group * ROWS, vectors * ROWS), half),
            VMEM((group, orbitals, orbitals), half),
            VMEM((n, *shape), half),
            VMEM((n, *shape), half),
            VMEM((n, *shape), half),
            VMEM((n, *shape), half),
            VMEM((n, *shape), half),
            VMEM((n, count, 8, 128), jnp.float32),
            VMEM((columns, *shape), jnp.float32),
            VMEM((columns, *shape), half),
            VMEM(shape, half),
            VMEM(shape, jnp.float32),
            pltpu.SemaphoreType.DMA((5, n - 1)),
            pltpu.SemaphoreType.DMA((5, n - 1)),
            pltpu.SemaphoreType.DMA((2, columns - 1)),
            pltpu.SemaphoreType.DMA((2, columns - 1)),
        ],
        compiler_params=pltpu.CompilerParams(
            collective_id=1, has_side_effects=True, vmem_limit_bytes=LIMIT
        ),
    )(
        fields,
        energy.reshape(n, count, 8, 128),
        walkers.astype(half),
        walkers,
        cholesky,
    )


def shards(walkers, inverse_intersection, half_rotated, cholesky, field_noise, branch_sources):
    count, occupied, orbitals = walkers.shape
    n = lax.axis_size("stretch")
    columns = lax.axis_size("walk")
    group = count * n
    green = gather_green(inverse_intersection, walkers, n)
    green = jnp.transpose(green.reshape(group, occupied, orbitals), (1, 0, 2))
    rotated = jnp.transpose(half_rotated, (1, 0, 2))
    force_bias, fields, energy = bias_and_energy(green, rotated, field_noise)
    column, energy = propagate(fields, energy, walkers, cholesky, n, columns)
    position = branch_sources // group * count + branch_sources % count
    picked = jnp.take(column.reshape(columns * count, occupied, orbitals), position, axis=0)
    return (force_bias, energy[:, 0, 0], picked)


def solution(mesh):
    placed = (
        P(("walk", "stretch"), None, None),
        P(("walk", "stretch"), None, None),
        P("stretch", None, None),
        P("stretch", None, None),
        P("walk", "stretch"),
        P(("walk", "stretch")),
    )
    return jax.shard_map(
        shards,
        mesh=mesh,
        in_specs=placed,
        out_specs=(
            P("walk", "stretch"),
            P(("walk", "stretch")),
            P(("walk", "stretch"), None, None),
        ),
        check_vma=False,
    )
```

```python
import functools
import math

import jax
import jax.numpy as jnp
from jax import lax
from jax.experimental import pallas as pl
from jax.experimental.pallas import tpu as pltpu
from jax.sharding import PartitionSpec as P

ORDERS = 2
ROWS = 16
MESH = pl.DeviceIdType.MESH
VMEM = pltpu.VMEM
LIMIT = 60 * 2**20


def around(axis, n, me, d):
    return {axis: lax.rem(me + d, n)}


def send(src, dst, sems, stage, d, device):
    return pltpu.make_async_remote_copy(
        src_ref=src,
        dst_ref=dst,
        send_sem=sems[0].at[stage, d - 1],
        recv_sem=sems[1].at[stage, d - 1],
        device_id=device,
        device_id_type=MESH,
    )


def greet(axes):
    barrier = pltpu.get_barrier_semaphore()
    total = 0
    for axis, n, me in axes:
        for d in range(1, n):
            pl.semaphore_signal(barrier, inc=1, device_id=around(axis, n, me, d), device_id_type=MESH)
        total += n - 1
    pl.semaphore_wait(barrier, total)


class Ring:
    def __init__(self, n, send_sem, recv_sem):
        self.n, self.line = n, n // 2
        self.me = lax.axis_index("stretch")
        self.parity = lax.rem(self.me, 2)
        self.at = self.me // 2
        self.pair = self.me + 1 - 2 * self.parity
        self.sems = (send_sem, recv_sem)

    def ahead(self, d):
        return lax.rem(self.at + d, self.line)

    def back(self, d):
        return lax.rem(self.at - d + self.line, self.line)

    def own(self, j):
        return 2 * j + self.parity

    def other(self, j):
        return 2 * j + 1 - self.parity

    def copy(self, src, dst, stage, slot, to):
        return send(src, dst, self.sems, stage, slot + 1, {"stretch": to})

    def along(self, buf, stage, d):
        return self.copy(buf.at[self.me], buf.at[self.me], stage, d - 1, self.own(self.ahead(d)))

    def across(self, buf, stage):
        return self.copy(buf.at[self.me], buf.at[self.me], stage, self.line - 1, self.pair)

    def forward(self, buf, stage, d):
        source = self.own(self.back(d))
        return self.copy(buf.at[source], buf.at[source], stage, self.line - 1 + d, self.pair)

    def gather_start(self, buf, stage):
        for d in range(1, self.line):
            self.along(buf, stage, d).start()
        self.across(buf, stage).start()

    def gather_forward(self, buf, stage):
        for d in range(1, self.line):
            self.along(buf, stage, d).wait_recv()
            self.forward(buf, stage, d).start()

    def gather_finish(self, buf, stage):
        for d in range(1, self.line):
            self.along(buf, stage, d).wait_send()
        self.across(buf, stage).wait()
        for d in range(1, self.line):
            self.forward(buf, stage, d).wait()

    def first(self, bufs, stage, d):
        j = self.ahead(d)
        return self.copy(bufs[0].at[j], bufs[1].at[j], stage, d, self.pair)

    def second(self, bufs, stage, d):
        j = self.ahead(d)
        return self.copy(
            bufs[2].at[j], bufs[3].at[self.at], stage, self.line + d - 1, self.own(j)
        )

    def scatter_first(self, bufs, stage, partial):
        for d in [*range(1, self.line), 0]:
            j = self.ahead(d)
            for k, value in enumerate(partial(self.other(j))):
                bufs[0][j, k] = value.astype(bufs[0].dtype)
            self.first(bufs, stage, d).start()

    def scatter_second(self, bufs, stage, partial, total):
        for d in [*range(1, self.line), 0]:
            j = self.ahead(d)
            values = partial(self.own(j))
            self.first(bufs, stage, d).wait()
            for k, value in enumerate(values):
                value = value + bufs[1][j, k].astype(jnp.float32)
                if d:
                    bufs[2][j, k] = value.astype(bufs[2].dtype)
                else:
                    total[k] = value
            if d:
                self.second(bufs, stage, d).start()

    def scatter_last(self, bufs, stage, total):
        for d in range(1, self.line):
            self.second(bufs, stage, d).wait()
            total[...] += bufs[3][self.back(d)].astype(jnp.float32)


def green_kernel(
    n, inverse_ref, walkers_ref, rotated_ref, out_ref, turned_ref, landed, send_sem, recv_sem
):
    ring = Ring(n, send_sem, recv_sem)
    vectors, occupied, orbitals = rotated_ref.shape
    per_vector = math.gcd(vectors, ROWS)

    def turn(low, high):
        @pl.loop(low, high)
        def _(g):
            start = pl.multiple_of(g * per_vector, per_vector)
            for i in range(0, occupied, ROWS):
                block = rotated_ref[pl.ds(start, per_vector), i : i + ROWS, :]
                turned_ref[i : i + ROWS, pl.ds(start, per_vector), :] = jnp.swapaxes(block, 0, 1)

    for k in range(walkers_ref.shape[0]):
        landed[ring.me, k] = jnp.dot(
            inverse_ref[k],
            walkers_ref[k],
            precision=lax.Precision.HIGHEST,
            preferred_element_type=jnp.float32,
        ).astype(jnp.bfloat16)
    greet([("stretch", n, ring.me)])
    ring.gather_start(landed, 0)
    blocks = vectors // per_vector
    turn(0, blocks // 2)
    ring.gather_forward(landed, 0)
    turn(blocks // 2, blocks)
    ring.gather_finish(landed, 0)
    count = walkers_ref.shape[0]
    several = math.gcd(n, ROWS // math.gcd(count, ROWS))
    block = several * count
    for b in range(n // several):
        for i in range(0, occupied, ROWS):
            part = landed[b * several : (b + 1) * several, :, i : i + ROWS, :]
            out_ref[i : i + ROWS, b * block : (b + 1) * block, :] = jnp.swapaxes(
                part.reshape(block, ROWS, orbitals), 0, 1
            )


def gather_green(inverse, walkers, rotated, n):
    shape = walkers.shape
    vectors, occupied, orbitals = rotated.shape
    return pl.pallas_call(
        functools.partial(green_kernel, n),
        out_shape=(
            jax.ShapeDtypeStruct((occupied, n * shape[0], orbitals), jnp.bfloat16),
            jax.ShapeDtypeStruct((occupied, vectors, orbitals), jnp.bfloat16),
        ),
        in_specs=[pl.BlockSpec(memory_space=VMEM)] * 3,
        out_specs=(pl.BlockSpec(memory_space=VMEM), pl.BlockSpec(memory_space=VMEM)),
        scratch_shapes=[
            VMEM((n, *shape), jnp.bfloat16),
            pltpu.SemaphoreType.DMA((1, n - 1)),
            pltpu.SemaphoreType.DMA((1, n - 1)),
        ],
        compiler_params=pltpu.CompilerParams(
            collective_id=0, has_side_effects=True, vmem_limit_bytes=LIMIT
        ),
    )(inverse, walkers, rotated)


def bias_kernel(green_ref, rotated_ref, noise_ref, bias_ref, fields_ref, energy_ref, inter):
    step = pl.program_id(1)
    occupied, block, orbitals = green_ref.shape
    span, vectors, _ = rotated_ref.shape
    green = green_ref[...].reshape(occupied * block, orbitals)
    for i in range(0, span, 2):
        part = lax.dot_general(
            green,
            rotated_ref[i : i + 2].reshape(2 * vectors, orbitals),
            (((1,), (1,)), ((), ())),
            preferred_element_type=jnp.float32,
        )
        for k in range(2):
            inter[step * span + i + k] = part[:, k * vectors : (k + 1) * vectors].reshape(
                occupied, block, vectors
            )

    @pl.when(step == pl.num_programs(1) - 1)
    def _():
        def one(i, carry):
            energy, trace = carry
            energy = energy + jnp.sum(inter[i] * inter[:, i], axis=0)
            return energy, trace + inter[i, i]

        zero = jnp.zeros((block, vectors), jnp.float32)
        energy, trace = lax.fori_loop(0, occupied, one, (zero, zero))
        bias = 2.0 * trace
        bias_ref[...] = bias
        fields_ref[...] = (0.05 * (noise_ref[...] - bias)).astype(jnp.bfloat16).astype(jnp.float32)
        share = -0.5 * jnp.sum(energy, axis=1, keepdims=True)
        energy_ref[...] = jnp.broadcast_to(share[:, :, None], energy_ref.shape)


def bias_and_energy(green, rotated, noise):
    occupied, group, orbitals = green.shape
    vectors = rotated.shape[1]
    block = math.gcd(group, 16)
    span = 8
    grid = (group // block, occupied // span)
    return pl.pallas_call(
        bias_kernel,
        grid=grid,
        out_shape=(
            jax.ShapeDtypeStruct((group, vectors), jnp.float32),
            jax.ShapeDtypeStruct((group, vectors), jnp.float32),
            jax.ShapeDtypeStruct((group, 8, 128), jnp.float32),
        ),
        in_specs=[
            pl.BlockSpec((occupied, block, orbitals), lambda w, i: (0, w, 0)),
            pl.BlockSpec((span, vectors, orbitals), lambda w, i: (i, 0, 0)),
            pl.BlockSpec((block, vectors), lambda w, i: (w, 0)),
        ],
        out_specs=(
            pl.BlockSpec((block, vectors), lambda w, i: (w, 0)),
            pl.BlockSpec((block, vectors), lambda w, i: (w, 0)),
            pl.BlockSpec((block, 8, 128), lambda w, i: (w, 0, 0)),
        ),
        scratch_shapes=[VMEM((occupied, occupied, block, vectors), jnp.float32)],
        compiler_params=pltpu.CompilerParams(vmem_limit_bytes=LIMIT),
    )(green, rotated, noise)


def propagate_kernel(
    n,
    columns,
    fields_ref,
    energy_in,
    rows_ref,
    walkers_ref,
    chol_ref,
    out_ref,
    energy_ref,
    spread,
    matrix,
    rows_all,
    rows_next,
    out_first,
    landed_first,
    out_second,
    landed_second,
    total,
    energy_landed,
    column_walkers,
    column_terms,
    terms,
    send_sem,
    recv_sem,
    column_send,
    column_recv,
):
    ring = Ring(n, send_sem, recv_sem)
    me = ring.me
    seat = lax.axis_index("walk")
    half, step = pl.program_id(0), pl.program_id(1)
    last = pl.num_programs(1) - 1
    vectors, span, width = chol_ref.shape
    group = fields_ref.shape[0]
    count = rows_ref.shape[0]
    column_sems = (column_send, column_recv)

    def at(h, p):
        return pl.when((half == h) & (step == p))

    def energy_copy(d):
        there = lax.rem(me + d, n)
        return ring.copy(energy_in.at[there], energy_landed.at[me], 1, d - 1, there)

    def column_copy(src, dst, stage, d):
        return send(
            src, dst.at[seat], column_sems, stage, d, around("walk", columns, seat, d)
        )

    def bufs(q):
        return (out_first.at[q], landed_first.at[q], out_second.at[q], landed_second.at[q])

    def order_one(h):
        def partial(owner):
            return [
                jnp.dot(
                    rows_all[owner, k],
                    matrix[h, owner * count + k],
                    preferred_element_type=jnp.float32,
                )
                for k in range(count)
            ]

        return partial

    def order_two(h):
        def one(owner, k):
            return 0.5 * sum(
                jnp.dot(
                    rows_next[g, owner, k],
                    matrix[h, owner * count + k, g * width : (g + 1) * width, :],
                    preferred_element_type=jnp.float32,
                )
                for g in range(2)
            )

        return lambda owner: [one(owner, k) for k in range(count)]

    @at(0, 0)
    def _():
        greet([("stretch", n, me), ("walk", columns, seat)])
        rows_all[me] = rows_ref[...]
        ring.gather_start(rows_all, 0)
        for d in range(1, n):
            energy_copy(d).start()
        for d in range(1, columns):
            column_copy(walkers_ref, column_walkers, 0, d).start()
        wide = vectors * ROWS
        column = lax.broadcasted_iota(jnp.int32, (vectors, wide), 1)
        row = lax.broadcasted_iota(jnp.int32, (vectors, wide), 0)
        repeat = jnp.where(column // ROWS == row, 1.0, 0.0).astype(jnp.bfloat16)
        repeated = jnp.dot(
            fields_ref[...].astype(jnp.bfloat16), repeat, preferred_element_type=jnp.float32
        )
        place = lax.broadcasted_iota(jnp.int32, (ROWS, wide), 0)
        where = lax.broadcasted_iota(jnp.int32, (ROWS, wide), 1) % ROWS
        for w in range(group):
            line = jnp.broadcast_to(repeated[w : w + 1], (ROWS, wide))
            spread[w * ROWS : (w + 1) * ROWS] = jnp.where(place == where, line, 0.0).astype(
                jnp.bfloat16
            )

    for c in range(span // ROWS):
        product = jnp.dot(
            spread[...],
            chol_ref[:, c * ROWS : (c + 1) * ROWS, :].reshape(vectors * ROWS, width),
            preferred_element_type=jnp.float32,
        )
        start = pl.multiple_of(step * span + c * ROWS, ROWS)
        matrix[half, :, pl.ds(start, ROWS), :] = product.astype(jnp.bfloat16).reshape(
            group, ROWS, width
        )

    @at(0, last // 2)
    def _():
        ring.gather_forward(rows_all, 0)

    @at(0, last)
    def _():
        ring.gather_finish(rows_all, 0)
        ring.scatter_first(bufs(0), 2, order_one(0))

    @at(1, last // 3)
    def _():
        ring.scatter_second(bufs(0), 2, order_one(0), total.at[0])

    @at(1, last // 3 * 2)
    def _():
        ring.scatter_last(bufs(0), 2, total.at[0])
        rows_next[0, me] = total[0].astype(jnp.bfloat16)
        ring.gather_start(rows_next.at[0], 4)

    @at(1, last - 1)
    def _():
        ring.gather_forward(rows_next.at[0], 4)

    @at(1, last)
    def _():
        ring.scatter_first(bufs(1), 3, order_one(1))
        ring.gather_finish(rows_next.at[0], 4)
        ring.scatter_second(bufs(1), 3, order_one(1), total.at[1])
        ring.scatter_last(bufs(1), 3, total.at[1])
        rows_next[1, me] = total[1].astype(jnp.bfloat16)
        ring.gather_start(rows_next.at[1], 5)
        for d in range(1, n):
            energy_copy(d).wait()
        energy = energy_in[me]
        for d in range(1, n):
            energy = energy + energy_landed[lax.rem(me - d + n, n)]
        energy_ref[...] = energy
        for d in range(1, columns):
            column_copy(walkers_ref, column_walkers, 0, d).wait()
        column_walkers[seat] = walkers_ref[...]
        ring.gather_forward(rows_next.at[1], 5)
        ring.gather_finish(rows_next.at[1], 5)
        for h in range(2):
            ring.scatter_first(bufs(2 + h), 6 + h, order_two(h))
        for h in range(2):
            ring.scatter_second(bufs(2 + h), 6 + h, order_two(h), total.at[2 + h])
        for h in range(2):
            ring.scatter_last(bufs(2 + h), 6 + h, total.at[2 + h])
            total[2 + h] += total[h]
            terms[h] = total[2 + h].astype(jnp.bfloat16)
            for d in range(1, columns):
                column_copy(terms.at[h], column_terms.at[h], 1 + h, d).start()
        for h in range(2):
            part = slice(h * width, (h + 1) * width)
            out_ref[seat, :, :, part] = walkers_ref[:, :, part] + total[2 + h]
            for d in range(1, columns):
                column_copy(terms.at[h], column_terms.at[h], 1 + h, d).wait()
                source = lax.rem(seat - d + columns, columns)
                out_ref[source, :, :, part] = column_walkers[source, :, :, part] + column_terms[
                    h, source
                ].astype(jnp.float32)


def propagate(fields, energy, walkers, cholesky, n, columns):
    count, occupied, orbitals = walkers.shape
    group, vectors = fields.shape
    span = 4 * ROWS
    width = orbitals // 2
    shape = (count, occupied, orbitals)
    part = (count, occupied, width)
    whole = pl.BlockSpec(memory_space=VMEM)
    half = jnp.bfloat16
    return pl.pallas_call(
        functools.partial(propagate_kernel, n, columns),
        grid=(2, orbitals // span),
        out_shape=(
            jax.ShapeDtypeStruct((columns, *shape), jnp.float32),
            jax.ShapeDtypeStruct((count, 8, 128), jnp.float32),
        ),
        in_specs=[
            whole,
            whole,
            whole,
            whole,
            pl.BlockSpec((vectors, span, width), lambda h, p: (0, p, h)),
        ],
        out_specs=(whole, whole),
        scratch_shapes=[
            VMEM((group * ROWS, vectors * ROWS), half),
            VMEM((2, group, orbitals, width), half),
            VMEM((n, *shape), half),
            VMEM((2, n, *part), half),
            VMEM((4, n // 2, *part), half),
            VMEM((4, n // 2, *part), half),
            VMEM((4, n // 2, *part), half),
            VMEM((4, n // 2, *part), half),
            VMEM((4, *part), jnp.float32),
            VMEM((n, count, 8, 128), jnp.float32),
            VMEM((columns, *shape), jnp.float32),
            VMEM((2, columns, *part), half),
            VMEM((2, *part), half),
            pltpu.SemaphoreType.DMA((8, n - 1)),
            pltpu.SemaphoreType.DMA((8, n - 1)),
            pltpu.SemaphoreType.DMA((3, columns - 1)),
            pltpu.SemaphoreType.DMA((3, columns - 1)),
        ],
        compiler_params=pltpu.CompilerParams(
            collective_id=1, has_side_effects=True, vmem_limit_bytes=LIMIT
        ),
    )(
        fields,
        energy.reshape(n, count, 8, 128),
        walkers.astype(half),
        walkers,
        cholesky,
    )


def shards(walkers, inverse_intersection, half_rotated, cholesky, field_noise, branch_sources):
    count, occupied, orbitals = walkers.shape
    n = lax.axis_size("stretch")
    columns = lax.axis_size("walk")
    group = count * n
    green, rotated = gather_green(inverse_intersection, walkers, half_rotated, n)
    force_bias, fields, energy = bias_and_energy(green, rotated, field_noise)
    column, energy = propagate(fields, energy, walkers, cholesky, n, columns)
    position = branch_sources // group * count + branch_sources % count
    column = column.reshape(columns * count, occupied, orbitals)
    picked = column.at[position].get(mode="promise_in_bounds")
    return (force_bias, energy[:, 0, 0], picked)


def solution(mesh):
    placed = (
        P(("walk", "stretch"), None, None),
        P(("walk", "stretch"), None, None),
        P("stretch", None, None),
        P("stretch", None, None),
        P("walk", "stretch"),
        P(("walk", "stretch")),
    )
    return jax.shard_map(
        shards,
        mesh=mesh,
        in_specs=placed,
        out_specs=(
            P("walk", "stretch"),
            P(("walk", "stretch")),
            P(("walk", "stretch"), None, None),
        ),
        check_vma=False,
    )
```
